32 devices in a mesh: src: 8 (over z, x), tgt: 4 (over y, core).
Axes of the slice: x: 2, y: 2, z: 4, core: 2. Of those that a mesh axis runs over, the one named last changes fastest.
Arguments:
- src_embed: float32 [16384, 256], P(('src', 'tgt')), may hold values from -7.5 to 7.5
- tgt_embed: float32 [16384, 256], P(('tgt', 'src')), may hold values from -7.5 to 7.5
- log_src: float32 [16384], P('src'), may hold values from -1.25 to 2.35
- log_tgt: float32 [16384], P('tgt'), may hold values from -1.25 to 2.35
- tgt_pot: float32 [16384], P('tgt'), may hold values from -1 to 6
Outputs:
- src_dual: float32 [16384], P('src')
- tgt_dual: float32 [16384], P('tgt')
The draws below stay inside these ranges and needn't reach their ends.
All inputs are finite; a program needn't handle non-finite values.
Results may differ from the reference program's by a relative error of at most 0.0003.
Values sent between devices are 32-bit elements; how exact they have to be, the bound alone decides.
A program may use at most 128 MiB of HBM per device.

```python
import math
import jax
import jax.numpy as jnp
from jax import lax

E = 256
COL_DEV = 4096
ITERS = 1
NS = 16384
NT = 16384


def draw_src_embed(key, part):
    main_key = jax.random.fold_in(key, 1)
    values = jnp.clip(jax.random.normal(main_key, (NS, E), jnp.float32), -4.0, 4.0)
    return values


def draw_tgt_embed(key, part):
    main_key = jax.random.fold_in(key, 2)
    values = jnp.clip(jax.random.normal(main_key, (NT, E), jnp.float32), -4.0, 4.0)
    return values


def mass_draw(key, count):
    ramp = jnp.log1p(2.0 * jnp.arange(count, dtype=jnp.float32) / count)
    noise = jax.random.uniform(key, (count,), jnp.float32, -1.2, 1.2)
    return noise + ramp


def draw_log_src(key, part):
    return mass_draw(jax.random.fold_in(key, 21), NS)


def draw_log_tgt(key, part):
    return mass_draw(jax.random.fold_in(key, 22), NT)


def draw_tgt_pot(key, part):
    own_key = jax.random.fold_in(key, 31)
    position = (jnp.arange(NT, dtype=jnp.int32) % COL_DEV).astype(jnp.float32) / COL_DEV
    noise = jax.random.uniform(own_key, (NT,), jnp.float32, -0.4, 0.4)
    values = jnp.clip(-1.0 + 7.0 * position + noise, -1.0, 6.0)
    return values


def setup_inputs(seed: int = 0) -> dict:
    key_list = jax.random.split(jax.random.key(seed), 6)
    src_embed = draw_src_embed(jax.random.fold_in(key_list[5], 71), 0)
    tgt_embed = draw_tgt_embed(jax.random.fold_in(key_list[5], 71), 0)
    log_src = draw_log_src(jax.random.fold_in(key_list[5], 71), 0)
    log_tgt = draw_log_tgt(jax.random.fold_in(key_list[5], 71), 0)
    tgt_pot = draw_tgt_pot(jax.random.fold_in(key_list[5], 71), 0)
    return dict(src_embed=src_embed, tgt_embed=tgt_embed, log_src=log_src, log_tgt=log_tgt, tgt_pot=tgt_pot)


EPSILON = 0.05


def reference(src_embed, tgt_embed, log_src, log_tgt, tgt_pot):
    block_rows = math.gcd(NS, 1024)
    block_count = NS // block_rows
    tgt_norm = jnp.sum(tgt_embed * tgt_embed, axis=1)
    tgt_dual = tgt_pot
    src_dual = jnp.zeros((NS,), jnp.float32)
    for turn in range(ITERS):
        def sweep(carry, index):
            highest, totals = carry
            first = (index * block_rows).astype(jnp.int32)
            rows = lax.dynamic_slice_in_dim(src_embed, first, block_rows, 0)
            masses = lax.dynamic_slice_in_dim(log_src, first, block_rows, 0)
            src_norm = jnp.sum(rows * rows, axis=1)
            inner = jnp.dot(rows, tgt_embed.T, precision=lax.Precision.HIGHEST, preferred_element_type=jnp.float32)
            cost = (src_norm[:, None] + tgt_norm[None, :] - 2.0 * inner) / E
            scores = log_tgt[None, :] + (tgt_dual[None, :] - cost) / EPSILON
            row_top = jnp.max(scores, axis=1)
            row_sum = jnp.sum(jnp.exp(scores - row_top[:, None]), axis=1)
            dual_block = -EPSILON * (row_top + jnp.log(row_sum))
            column = masses[:, None] + (dual_block[:, None] - cost) / EPSILON
            column_top = jnp.maximum(highest, jnp.max(column, axis=0))
            totals = totals * jnp.exp(highest - column_top) + jnp.sum(jnp.exp(column - column_top[None, :]), axis=0)
            return (column_top, totals), dual_block

        start = (jnp.full((NT,), -jnp.inf, jnp.float32), jnp.zeros((NT,), jnp.float32))
        (column_top, totals), blocks = lax.scan(sweep, start, jnp.arange(block_count, dtype=jnp.int32))
        src_dual = blocks.reshape(NS)
        tgt_dual = -EPSILON * (column_top + jnp.log(totals))
    return src_dual, tgt_dual
```

```python
import functools
import math

import jax
import jax.numpy as jnp
from jax import lax
from jax.experimental import pallas as pl
from jax.experimental.pallas import tpu as pltpu
from jax.sharding import PartitionSpec as P

EPSILON = 0.05
LOG2E = math.log2(math.e)
LN2 = math.log(2.0)
LOW = -1e38
LANES = 128
CHUNKS = 2


def ring_place(src, wide, deep):
    z, x = src // wide, src % wide
    return x * deep + jnp.where(x % 2 == 0, z, deep - 1 - z)


def ring_owner(place, wide, deep):
    x, step = place // deep, place % deep
    z = jnp.where(x % 2 == 0, step, deep - 1 - step)
    return z * wide + x


def across(column, count):
    return jnp.concatenate([column] * (count // LANES), axis=1)


def upright(row):
    return jnp.transpose(jnp.broadcast_to(row, (LANES, row.shape[1])))


def flat(columns):
    return jnp.transpose(columns)[0:1, :]


def halves(values):
    high = values.astype(jnp.bfloat16)
    low = (values - high.astype(jnp.float32)).astype(jnp.bfloat16)
    return high, low


def contract(left, right):
    return lax.dot_general(
        left, right, (((1,), (1,)), ((), ())), preferred_element_type=jnp.float32
    )


def combine(parts, count):
    top = functools.reduce(jnp.maximum, [parts[k] for k in range(count)])
    total = sum(jnp.exp2(parts[k] - top) for k in range(count))
    return top + jnp.log2(total)


def kernel(
    n_src, n_tgt, wide, deep,
    x_own, y_own, log_src, log_tgt, pot, src_out, tgt_out,
    x_all, y_all, x_ops, y_ops, a_col, b_col, x_norm, y_norm,
    row_top, row_sum, row_parts, col_parts,
    ring_send, ring_recv, y_send, y_recv, core_send, core_recv,
    row_send, row_recv, col_send, col_recv,
):
    s = lax.axis_index("src")
    t = lax.axis_index("tgt")
    n_y = n_tgt // 2
    y_me, core = t // 2, t % 2
    partner = y_me * 2 + 1 - core
    place = ring_place(s, wide, deep)
    after = ring_owner((place + 1) % n_src, wide, deep)
    before = ring_owner((place + n_src - 1) % n_src, wide, deep)
    xb, width = x_own.shape
    yb = y_own.shape[0]
    rows, cols = n_tgt * xb, n_src * yb
    half = yb // 2
    part = half // CHUNKS
    scale = 1.0 / (width * EPSILON)

    barrier = pltpu.get_barrier_semaphore()
    for d in range(1, n_tgt):
        pl.semaphore_signal(
            barrier, inc=1, device_id={"tgt": (t + d) % n_tgt}, device_id_type=pl.DeviceIdType.MESH
        )

    def greet(d, carry):
        pl.semaphore_signal(
            barrier, inc=1, device_id={"src": (s + d) % n_src}, device_id_type=pl.DeviceIdType.MESH
        )
        return carry

    lax.fori_loop(1, n_src, greet, 0)
    pl.semaphore_wait(barrier, n_src + n_tgt - 2)

    def owner_of(k, way):
        return ring_owner((place + n_src + (k if way else -k)) % n_src, wide, deep)

    def ring_copy(k, way, c, first=False):
        offset = way * half + c * part
        sent = pl.multiple_of(owner_of(k - 1, way) * yb + offset, part)
        source = y_own.at[pl.ds(offset, part)] if first else y_all.at[pl.ds(sent, part)]
        return pltpu.make_async_remote_copy(
            src_ref=source,
            dst_ref=y_all.at[pl.ds(sent, part)],
            send_sem=ring_send.at[k, way, c],
            recv_sem=ring_recv.at[k, way, c],
            device_id={"src": before if way else after},
            device_id_type=pl.DeviceIdType.MESH,
        )

    def ring_arrival(k, way, c):
        offset = way * half + c * part
        got = pl.multiple_of(owner_of(k, way) * yb + offset, part)
        return pltpu.make_async_remote_copy(
            src_ref=y_all.at[pl.ds(got, part)],
            dst_ref=y_all.at[pl.ds(got, part)],
            send_sem=ring_send.at[k, way, c],
            recv_sem=ring_recv.at[k, way, c],
            device_id={"src": before if way else after},
            device_id_type=pl.DeviceIdType.MESH,
        )

    def x_copy(source, slot, send, recv, target):
        return pltpu.make_async_remote_copy(
            src_ref=source,
            dst_ref=x_all.at[slot],
            send_sem=send,
            recv_sem=recv,
            device_id={"tgt": target},
            device_id_type=pl.DeviceIdType.MESH,
        )

    order = [(way, c) for c in range(CHUNKS) for way in range(2)]
    for way, c in order:
        ring_copy(1, way, c, first=True).start()
    for d in range(1, n_y):
        target = ((y_me + d) % n_y) * 2 + core
        x_copy(x_own, t, y_send.at[d], y_recv.at[d], target).start()
    x_copy(x_own, t, core_send.at[0], core_recv.at[0], partner).start()

    a_col[...] = upright((log_tgt[...] + pot[...] / EPSILON) * LOG2E)
    row_top[...] = jnp.full_like(row_top, LOW)
    row_sum[...] = jnp.zeros_like(row_sum)

    def prepare_x(slot, values):
        where = pl.ds(pl.multiple_of(slot * xb, xb), xb)
        x_norm[where, :] = jnp.broadcast_to(jnp.sum(values * values, axis=1, keepdims=True), (xb, LANES))
        high, low = halves(values * (2.0 * scale * LOG2E))
        x_ops[where, 0:width] = high
        x_ops[where, width : 2 * width] = low
        x_ops[where, 2 * width : 3 * width] = high

    def prepare_y(first, values):
        where = pl.ds(first, half)
        norm = jnp.broadcast_to(jnp.sum(values * values, axis=1, keepdims=True), (half, LANES))
        y_norm[where, :] = norm
        a_col[where, :] = a_col[where, :] - norm * (scale * LOG2E)
        high, low = halves(values)
        y_ops[where, 0:width] = high
        y_ops[where, width : 2 * width] = high
        y_ops[where, 2 * width : 3 * width] = low

    prepare_x(t, x_own[...])
    for way in range(2):
        here = pl.multiple_of(s * yb + way * half, half)
        prepare_y(here, y_own[way * half : (way + 1) * half, :])

    def pass_on(k, carry):
        for way, c in order:
            ring_arrival(k, way, c).wait_recv()

            @pl.when(k < n_src - 1)
            def _():
                ring_copy(k + 1, way, c).start()

        for way in range(2):
            here = pl.multiple_of(owner_of(k, way) * yb + way * half, half)
            prepare_y(here, y_all[pl.ds(here, half), :])
        return carry

    lax.fori_loop(1, 3, pass_on, 0)

    for d in range(1, n_y):
        slot = ((y_me + n_y - d) % n_y) * 2 + core
        x_copy(x_all.at[slot], slot, y_send.at[d], y_recv.at[d], partner).wait_recv()
        x_copy(x_all.at[slot], slot, core_send.at[d], core_recv.at[d], partner).start()
        prepare_x(slot, x_all[slot])
    for d in range(n_y):
        slot = ((y_me + n_y - d) % n_y) * 2 + 1 - core
        x_copy(x_all.at[slot], slot, core_send.at[d], core_recv.at[d], partner).wait_recv()
        prepare_x(slot, x_all[slot])

    wide_rows = min(512, rows)

    def row_sweep(k, carry):
        for way in range(2):
            here = pl.ds(pl.multiple_of(owner_of(k, way) * yb + way * half, half), half)
            left = y_ops[here, :]
            bias = across(a_col[here, :], wide_rows)
            for first in range(0, rows, wide_rows):
                span = slice(first, first + wide_rows)
                scores = contract(left, x_ops[span, :]) + bias
                old = row_top[:, span]
                top = jnp.maximum(old, jnp.max(scores, axis=0, keepdims=True))
                total = jnp.sum(jnp.exp2(scores - top), axis=0, keepdims=True)
                row_sum[:, span] = row_sum[:, span] * jnp.exp2(old - top) + total
                row_top[:, span] = top
        return carry

    def turn(k, carry):
        pass_on(k, 0)
        lax.fori_loop(jnp.minimum(2 * (k - 3), k), jnp.minimum(2 * (k - 2), k + 1), row_sweep, 0)
        return carry

    lax.fori_loop(3, n_src, turn, 0)

    def row_copy(d, slot):
        return pltpu.make_async_remote_copy(
            src_ref=row_parts.at[slot],
            dst_ref=row_parts.at[slot],
            send_sem=row_send.at[d],
            recv_sem=row_recv.at[d],
            device_id={"tgt": (t + d) % n_tgt},
            device_id_type=pl.DeviceIdType.MESH,
        )

    row_parts[t] = row_top[...] + jnp.log2(row_sum[...])
    for d in range(1, n_tgt):
        row_copy(d, t).start()
    norms = flat(x_norm[...])
    for d in range(1, n_tgt):
        row_copy(d, (t + n_tgt - d) % n_tgt).wait_recv()
    lse = combine(row_parts, n_tgt)
    b_col[...] = upright(log_src[...] * LOG2E - lse)
    src_out[...] = norms / width - (EPSILON * LN2) * lse

    wide_cols = min(512, cols)

    def column_sweep(index, carry):
        span = pl.ds(pl.multiple_of(index * wide_cols, wide_cols), wide_cols)
        right = y_ops[span, :]
        top = jnp.full((1, wide_cols), LOW, jnp.float32)
        total = jnp.zeros((1, wide_cols), jnp.float32)
        for first in range(0, rows, wide_rows):
            here = slice(first, first + wide_rows)
            scores = contract(x_ops[here, :], right) + across(b_col[here, :], wide_cols)
            old = top
            top = jnp.maximum(old, jnp.max(scores, axis=0, keepdims=True))
            total = total * jnp.exp2(old - top) + jnp.sum(jnp.exp2(scores - top), axis=0, keepdims=True)
        col_parts[s, :, span] = top + jnp.log2(total)
        return carry

    lax.fori_loop(0, cols // wide_cols, column_sweep, 0)

    def col_copy(d, slot):
        return pltpu.make_async_remote_copy(
            src_ref=col_parts.at[slot],
            dst_ref=col_parts.at[slot],
            send_sem=col_send.at[d],
            recv_sem=col_recv.at[d],
            device_id={"src": (s + d) % n_src},
            device_id_type=pl.DeviceIdType.MESH,
        )

    def send_columns(d, carry):
        col_copy(d, s).start()
        return carry

    def take_columns(d, carry):
        col_copy(d, (s + n_src - d) % n_src).wait_recv()
        return carry

    lax.fori_loop(1, n_src, send_columns, 0)
    norms = flat(y_norm[...])
    lax.fori_loop(1, n_src, take_columns, 0)
    tgt_out[...] = norms / width - (EPSILON * LN2) * combine(col_parts, n_src)

    def settle_ring(k, carry):
        for way, c in order:
            ring_copy(k, way, c).wait_send()
        return carry

    def settle_columns(d, carry):
        col_copy(d, s).wait_send()
        return carry

    lax.fori_loop(1, n_src, settle_ring, 0)
    lax.fori_loop(1, n_src, settle_columns, 0)
    for d in range(1, n_y):
        x_copy(x_own, t, y_send.at[d], y_recv.at[d], partner).wait_send()
    for d in range(n_y):
        x_copy(x_own, t, core_send.at[d], core_recv.at[d], partner).wait_send()
    for d in range(1, n_tgt):
        row_copy(d, t).wait_send()


def shards(n_src, n_tgt, src_embed, tgt_embed, log_src, log_tgt, tgt_pot):
    xb, width = src_embed.shape
    yb = tgt_embed.shape[0]
    rows, cols = n_tgt * xb, n_src * yb
    wide = max(w for w in range(1, n_src + 1) if n_src % w == 0 and 2 * w * w <= n_src)
    deep = n_src // wide
    sem = pltpu.SemaphoreType.DMA
    vmem = pl.BlockSpec(memory_space=pltpu.VMEM)
    f32, bf16 = jnp.float32, jnp.bfloat16
    src_dual, tgt_dual = pl.pallas_call(
        functools.partial(kernel, n_src, n_tgt, wide, deep),
        out_shape=(jax.ShapeDtypeStruct((1, rows), f32), jax.ShapeDtypeStruct((1, cols), f32)),
        in_specs=[vmem] * 5,
        out_specs=(vmem, vmem),
        scratch_shapes=[
            pltpu.VMEM((n_tgt, xb, width), f32),
            pltpu.VMEM((cols, width), f32),
            pltpu.VMEM((rows, 3 * width), bf16),
            pltpu.VMEM((cols, 3 * width), bf16),
            pltpu.VMEM((cols, LANES), f32),
            pltpu.VMEM((rows, LANES), f32),
            pltpu.VMEM((rows, LANES), f32),
            pltpu.VMEM((cols, LANES), f32),
            pltpu.VMEM((1, rows), f32),
            pltpu.VMEM((1, rows), f32),
            pltpu.VMEM((n_tgt, 1, rows), f32),
            pltpu.VMEM((n_src, 1, cols), f32),
            sem((n_src, 2, CHUNKS)),
            sem((n_src, 2, CHUNKS)),
            sem((n_tgt // 2,)),
            sem((n_tgt // 2,)),
            sem((n_tgt // 2,)),
            sem((n_tgt // 2,)),
            sem((n_tgt,)),
            sem((n_tgt,)),
            sem((n_src,)),
            sem((n_src,)),
        ],
        compiler_params=pltpu.CompilerParams(
            collective_id=0, has_side_effects=True, vmem_limit_bytes=52 * 1024 * 1024
        ),
        cost_estimate=pl.CostEstimate(
            flops=12 * rows * cols * width,
            bytes_accessed=4 * (rows + cols) * width,
            transcendentals=2 * rows * cols,
        ),
    )(src_embed, tgt_embed, log_src[None, :], log_tgt[None, :], tgt_pot[None, :])
    return src_dual.reshape(rows), tgt_dual.reshape(cols)


def solution(mesh):
    in_specs = (P(("src", "tgt"), None), P(("tgt", "src"), None), P("src"), P("tgt"), P("tgt"))
    out_specs = (P("src"), P("tgt"))
    body = functools.partial(shards, mesh.shape["src"], mesh.shape["tgt"])
    return jax.shard_map(body, mesh=mesh, in_specs=in_specs, out_specs=out_specs, check_vma=False)
```

```python
import functools
import math

import jax
import jax.numpy as jnp
from jax import lax
from jax.experimental import pallas as pl
from jax.experimental.pallas import tpu as pltpu
from jax.sharding import PartitionSpec as P

EPSILON = 0.05
LOG2E = math.log2(math.e)
LN2 = math.log(2.0)
LOW = -1e38
LANES = 128
CHUNKS = 2


def ring_place(src, wide, deep):
    z, x = src // wide, src % wide
    return x * deep + jnp.where(x % 2 == 0, z, deep - 1 - z)


def ring_owner(place, wide, deep):
    x, step = place // deep, place % deep
    z = jnp.where(x % 2 == 0, step, deep - 1 - step)
    return z * wide + x


def across(column, count):
    return jnp.concatenate([column] * (count // LANES), axis=1)


def upright(row):
    return jnp.transpose(jnp.broadcast_to(row, (LANES, row.shape[1])))


def flat(columns):
    return jnp.transpose(columns)[0:1, :]


def halves(values):
    high = values.astype(jnp.bfloat16)
    low = (values - high.astype(jnp.float32)).astype(jnp.bfloat16)
    return high, low


def contract(left, right):
    return lax.dot_general(
        left, right, (((1,), (1,)), ((), ())), preferred_element_type=jnp.float32
    )


def combine(parts, count):
    top = functools.reduce(jnp.maximum, [parts[k] for k in range(count)])
    total = sum(jnp.exp2(parts[k] - top) for k in range(count))
    return top + jnp.log2(total)


def kernel(
    n_src, n_tgt, wide, deep,
    x_own, y_own, log_src_in, log_tgt_in, pot_in, src_out, tgt_out,
    x_all, y_all, x_ops, products, a_col, b_rows, x_norm, y_norm,
    log_src, log_tgt, pot, row_top, row_sum, row_parts, col_parts,
    ring_send, ring_recv, y_send, y_recv, core_send, core_recv,
    row_send, row_recv, col_send, col_recv, local,
):
    s = lax.axis_index("src")
    t = lax.axis_index("tgt")
    n_y = n_tgt // 2
    y_me, core = t // 2, t % 2
    partner = y_me * 2 + 1 - core
    place = ring_place(s, wide, deep)
    after = ring_owner((place + 1) % n_src, wide, deep)
    before = ring_owner((place + n_src - 1) % n_src, wide, deep)
    xb, width = x_own.shape
    yb = y_own.shape[0]
    rows, cols = n_tgt * xb, n_src * yb
    half = yb // 2
    part = half // CHUNKS
    scale = 1.0 / (width * EPSILON)

    own_rows = pl.ds(pl.multiple_of(s * yb, yb), yb)
    own = [
        pltpu.make_async_copy(log_tgt_in, log_tgt, local.at[0]),
        pltpu.make_async_copy(pot_in, pot, local.at[1]),
        pltpu.make_async_copy(x_own, x_all.at[t], local.at[2]),
        pltpu.make_async_copy(y_own, y_all.at[own_rows], local.at[3]),
        pltpu.make_async_copy(log_src_in, log_src, local.at[4]),
    ]
    for copy in own:
        copy.start()

    barrier = pltpu.get_barrier_semaphore()
    for d in range(1, n_tgt):
        pl.semaphore_signal(
            barrier, inc=1, device_id={"tgt": (t + d) % n_tgt}, device_id_type=pl.DeviceIdType.MESH
        )

    def greet(d, carry):
        pl.semaphore_signal(
            barrier, inc=1, device_id={"src": (s + d) % n_src}, device_id_type=pl.DeviceIdType.MESH
        )
        return carry

    lax.fori_loop(1, n_src, greet, 0)
    pl.semaphore_wait(barrier, n_src + n_tgt - 2)

    def owner_of(k, way):
        return ring_owner((place + n_src + (k if way else -k)) % n_src, wide, deep)

    def ring_copy(k, way, c, first=False):
        offset = way * half + c * part
        sent = pl.multiple_of(owner_of(k - 1, way) * yb + offset, part)
        source = y_own.at[pl.ds(offset, part)] if first else y_all.at[pl.ds(sent, part)]
        return pltpu.make_async_remote_copy(
            src_ref=source,
            dst_ref=y_all.at[pl.ds(sent, part)],
            send_sem=ring_send.at[k, way, c],
            recv_sem=ring_recv.at[k, way, c],
            device_id={"src": before if way else after},
            device_id_type=pl.DeviceIdType.MESH,
        )

    def ring_arrival(k, way, c):
        offset = way * half + c * part
        got = pl.multiple_of(owner_of(k, way) * yb + offset, part)
        return pltpu.make_async_remote_copy(
            src_ref=y_all.at[pl.ds(got, part)],
            dst_ref=y_all.at[pl.ds(got, part)],
            send_sem=ring_send.at[k, way, c],
            recv_sem=ring_recv.at[k, way, c],
            device_id={"src": before if way else after},
            device_id_type=pl.DeviceIdType.MESH,
        )

    def x_copy(source, slot, send, recv, target):
        return pltpu.make_async_remote_copy(
            src_ref=source,
            dst_ref=x_all.at[slot],
            send_sem=send,
            recv_sem=recv,
            device_id={"tgt": target},
            device_id_type=pl.DeviceIdType.MESH,
        )

    order = [(way, c) for c in range(CHUNKS) for way in range(2)]
    for way, c in order:
        ring_copy(1, way, c, first=True).start()
    for d in range(1, n_y):
        target = ((y_me + d) % n_y) * 2 + core
        x_copy(x_own, t, y_send.at[d], y_recv.at[d], target).start()
    x_copy(x_own, t, core_send.at[0], core_recv.at[0], partner).start()

    for copy in own:
        copy.wait()
    a_col[...] = upright((log_tgt[...] + pot[...] / EPSILON) * LOG2E)
    row_top[...] = jnp.full_like(row_top, LOW)
    row_sum[...] = jnp.zeros_like(row_sum)

    def prepare_x(slot, values):
        where = pl.ds(pl.multiple_of(slot * xb, xb), xb)
        x_norm[where, :] = jnp.broadcast_to(jnp.sum(values * values, axis=1, keepdims=True), (xb, LANES))
        high, low = halves(values * (2.0 * scale * LOG2E))
        x_ops[where, 0:width] = high
        x_ops[where, width : 2 * width] = low
        x_ops[where, 2 * width : 3 * width] = high

    prepare_x(t, x_all[t])

    def pass_on(k, c):
        for way in range(2):
            ring_arrival(k, way, c).wait_recv()

            @pl.when(k < n_src - 1)
            def _():
                ring_copy(k + 1, way, c).start()

    def first_turns(k, carry):
        for c in range(CHUNKS):
            pass_on(k, c)
        return carry

    lax.fori_loop(1, 3, first_turns, 0)

    for d in range(1, n_y):
        slot = ((y_me + n_y - d) % n_y) * 2 + core
        x_copy(x_all.at[slot], slot, y_send.at[d], y_recv.at[d], partner).wait_recv()
        x_copy(x_all.at[slot], slot, core_send.at[d], core_recv.at[d], partner).start()
        prepare_x(slot, x_all[slot])
    for d in range(n_y):
        slot = ((y_me + n_y - d) % n_y) * 2 + 1 - core
        x_copy(x_all.at[slot], slot, core_send.at[d], core_recv.at[d], partner).wait_recv()
        prepare_x(slot, x_all[slot])

    wide_rows = min(512, rows)

    def row_sweep(k, carry):
        for way in range(2):
            here = pl.ds(pl.multiple_of(owner_of(k, way) * yb + way * half, half), half)
            values = y_all[here, :]
            norm = jnp.broadcast_to(jnp.sum(values * values, axis=1, keepdims=True), (half, LANES))
            y_norm[here, :] = norm
            bias = across(a_col[here, :] - norm * (scale * LOG2E), wide_rows)
            high, low = halves(values)
            left = jnp.concatenate([high, high, low], axis=1)
            for first in range(0, rows, wide_rows):
                span = slice(first, first + wide_rows)
                product = contract(left, x_ops[span, :])
                products[here, span] = product
                scores = product + bias
                old = row_top[:, span]
                top = jnp.maximum(old, jnp.max(scores, axis=0, keepdims=True))
                total = jnp.sum(jnp.exp2(scores - top), axis=0, keepdims=True)
                row_sum[:, span] = row_sum[:, span] * jnp.exp2(old - top) + total
                row_top[:, span] = top
        return carry

    def turn(k, carry):
        pass_on(k, 0)
        done = jnp.minimum(2 * (k - 3), k)
        ready = jnp.minimum(2 * (k - 3) + 1, k)
        lax.fori_loop(done, ready, row_sweep, 0)
        pass_on(k, 1)
        lax.fori_loop(ready, jnp.minimum(2 * (k - 2), k + 1), row_sweep, 0)
        return carry

    lax.fori_loop(3, n_src, turn, 0)

    def row_copy(d, slot):
        return pltpu.make_async_remote_copy(
            src_ref=row_parts.at[slot],
            dst_ref=row_parts.at[slot],
            send_sem=row_send.at[d],
            recv_sem=row_recv.at[d],
            device_id={"tgt": (t + d) % n_tgt},
            device_id_type=pl.DeviceIdType.MESH,
        )

    row_parts[t] = row_top[...] + jnp.log2(row_sum[...])
    for d in range(1, n_tgt):
        row_copy(d, t).start()
    norms = flat(x_norm[...])
    for d in range(1, n_tgt):
        row_copy(d, (t + n_tgt - d) % n_tgt).wait_recv()
    lse = combine(row_parts, n_tgt)
    b_rows[...] = jnp.broadcast_to(log_src[...] * LOG2E - lse, b_rows.shape)
    src_out[...] = norms / width - (EPSILON * LN2) * lse

    group = min(256, cols)

    def column_sweep(index, carry):
        begin = pl.multiple_of(index * group, group)
        tops, totals = [], []
        for first in range(0, group, 8):
            here = pl.ds(pl.multiple_of(begin + first, 8), 8)
            scores = [
                products[here, at : at + LANES] + b_rows[:, at : at + LANES]
                for at in range(0, rows, LANES)
            ]
            top = functools.reduce(jnp.maximum, scores)
            tops.append(top)
            totals.append(sum(jnp.exp2(score - top) for score in scores))
        lane_top = jnp.transpose(jnp.concatenate(tops, axis=0))
        lane_total = jnp.transpose(jnp.concatenate(totals, axis=0))
        top = jnp.max(lane_top, axis=0, keepdims=True)
        total = jnp.sum(lane_total * jnp.exp2(lane_top - top), axis=0, keepdims=True)
        col_parts[s, :, pl.ds(begin, group)] = top + jnp.log2(total)
        return carry

    lax.fori_loop(0, cols // group, column_sweep, 0)

    def col_copy(d, slot):
        return pltpu.make_async_remote_copy(
            src_ref=col_parts.at[slot],
            dst_ref=col_parts.at[slot],
            send_sem=col_send.at[d],
            recv_sem=col_recv.at[d],
            device_id={"src": (s + d) % n_src},
            device_id_type=pl.DeviceIdType.MESH,
        )

    def send_columns(d, carry):
        col_copy(d, s).start()
        return carry

    def take_columns(d, carry):
        col_copy(d, (s + n_src - d) % n_src).wait_recv()
        return carry

    lax.fori_loop(1, n_src, send_columns, 0)
    norms = flat(y_norm[...])
    lax.fori_loop(1, n_src, take_columns, 0)
    tgt_out[...] = norms / width - (EPSILON * LN2) * combine(col_parts, n_src)

    def settle_ring(k, carry):
        for way, c in order:
            ring_copy(k, way, c).wait_send()
        return carry

    def settle_columns(d, carry):
        col_copy(d, s).wait_send()
        return carry

    lax.fori_loop(1, n_src, settle_ring, 0)
    lax.fori_loop(1, n_src, settle_columns, 0)
    for d in range(1, n_y):
        x_copy(x_all.at[t], t, y_send.at[d], y_recv.at[d], partner).wait_send()
    for d in range(n_y):
        x_copy(x_all.at[t], t, core_send.at[d], core_recv.at[d], partner).wait_send()
    for d in range(1, n_tgt):
        row_copy(d, t).wait_send()


def shards(n_src, n_tgt, src_embed, tgt_embed, log_src, log_tgt, tgt_pot):
    xb, width = src_embed.shape
    yb = tgt_embed.shape[0]
    rows, cols = n_tgt * xb, n_src * yb
    wide = max(w for w in range(1, n_src + 1) if n_src % w == 0 and 2 * w * w <= n_src)
    deep = n_src // wide
    sem = pltpu.SemaphoreType.DMA
    vmem = pl.BlockSpec(memory_space=pltpu.VMEM)
    f32, bf16 = jnp.float32, jnp.bfloat16
    src_dual, tgt_dual = pl.pallas_call(
        functools.partial(kernel, n_src, n_tgt, wide, deep),
        out_shape=(jax.ShapeDtypeStruct((1, rows), f32), jax.ShapeDtypeStruct((1, cols), f32)),
        in_specs=[pl.BlockSpec(memory_space=pl.ANY)] * 5,
        out_specs=(vmem, vmem),
        scratch_shapes=[
            pltpu.VMEM((n_tgt, xb, width), f32),
            pltpu.VMEM((cols, width), f32),
            pltpu.VMEM((rows, 3 * width), bf16),
            pltpu.VMEM((cols, rows), f32),
            pltpu.VMEM((cols, LANES), f32),
            pltpu.VMEM((8, rows), f32),
            pltpu.VMEM((rows, LANES), f32),
            pltpu.VMEM((cols, LANES), f32),
            pltpu.VMEM((1, rows), f32),
            pltpu.VMEM((1, cols), f32),
            pltpu.VMEM((1, cols), f32),
            pltpu.VMEM((1, rows), f32),
            pltpu.VMEM((1, rows), f32),
            pltpu.VMEM((n_tgt, 1, rows), f32),
            pltpu.VMEM((n_src, 1, cols), f32),
            sem((n_src, 2, CHUNKS)),
            sem((n_src, 2, CHUNKS)),
            sem((n_tgt // 2,)),
            sem((n_tgt // 2,)),
            sem((n_tgt // 2,)),
            sem((n_tgt // 2,)),
            sem((n_tgt,)),
            sem((n_tgt,)),
            sem((n_src,)),
            sem((n_src,)),
            sem((5,)),
        ],
        compiler_params=pltpu.CompilerParams(
            collective_id=0, has_side_effects=True, vmem_limit_bytes=60 * 1024 * 1024
        ),
        cost_estimate=pl.CostEstimate(
            flops=6 * rows * cols * width,
            bytes_accessed=4 * (rows + cols) * width,
            transcendentals=2 * rows * cols,
        ),
    )(src_embed, tgt_embed, log_src[None, :], log_tgt[None, :], tgt_pot[None, :])
    return src_dual.reshape(rows), tgt_dual.reshape(cols)


def solution(mesh):
    in_specs = (P(("src", "tgt"), None), P(("tgt", "src"), None), P("src"), P("tgt"), P("tgt"))
    out_specs = (P("src"), P("tgt"))
    body = functools.partial(shards, mesh.shape["src"], mesh.shape["tgt"])
    return jax.shard_map(body, mesh=mesh, in_specs=in_specs, out_specs=out_specs, check_vma=False)
```

```python
import functools
import math

import jax
import jax.numpy as jnp
from jax import lax
from jax.experimental import pallas as pl
from jax.experimental.pallas import tpu as pltpu
from jax.sharding import PartitionSpec as P

EPSILON = 0.05
LOG2E = math.log2(math.e)
LN2 = math.log(2.0)
LOW = -1e38
LANES = 128
CHUNKS = 4
PARTS = 2


def ring_place(src, wide, deep):
    z, x = src // wide, src % wide
    return x * deep + jnp.where(x % 2 == 0, z, deep - 1 - z)


def ring_owner(place, wide, deep):
    x, step = place // deep, place % deep
    z = jnp.where(x % 2 == 0, step, deep - 1 - step)
    return z * wide + x


def across(column, count):
    return jnp.concatenate([column] * (count // LANES), axis=1)


def upright(row):
    return jnp.transpose(jnp.broadcast_to(row, (LANES, row.shape[1])))


def flat(columns):
    return jnp.transpose(columns)[0:1, :]


def halves(values):
    high = values.astype(jnp.bfloat16)
    low = (values - high.astype(jnp.float32)).astype(jnp.bfloat16)
    return high, low


def contract(left, right):
    return lax.dot_general(
        left, right, (((1,), (1,)), ((), ())), preferred_element_type=jnp.float32
    )


def combine(parts, count):
    top = functools.reduce(jnp.maximum, [parts[k] for k in range(count)])
    total = sum(jnp.exp2(parts[k] - top) for k in range(count))
    return top + jnp.log2(total)


def kernel(
    n_src, n_tgt, wide, deep,
    x_own, y_own, log_src_in, log_tgt_in, pot_in, src_out, tgt_out,
    x_all, y_all, x_ops, products, a_col, b_rows, x_norm, y_norm,
    log_src, log_tgt, pot, row_top, row_sum, row_parts, col_parts,
    ring_send, ring_recv, y_send, y_recv, core_send, core_recv,
    row_send, row_recv, col_send, col_recv, local,
):
    s = lax.axis_index("src")
    t = lax.axis_index("tgt")
    n_y = n_tgt // 2
    y_me, core = t // 2, t % 2
    partner = y_me * 2 + 1 - core
    place = ring_place(s, wide, deep)
    after = ring_owner((place + 1) % n_src, wide, deep)
    before = ring_owner((place + n_src - 1) % n_src, wide, deep)
    xb, width = x_own.shape
    yb = y_own.shape[0]
    rows, cols = n_tgt * xb, n_src * yb
    half = yb // 2
    part = half // CHUNKS
    scale = 1.0 / (width * EPSILON)

    own_rows = pl.ds(pl.multiple_of(s * yb, yb), yb)
    own = [
        pltpu.make_async_copy(log_tgt_in, log_tgt, local.at[0]),
        pltpu.make_async_copy(pot_in, pot, local.at[1]),
        pltpu.make_async_copy(x_own, x_all.at[t], local.at[2]),
        pltpu.make_async_copy(y_own, y_all.at[own_rows], local.at[3]),
        pltpu.make_async_copy(log_src_in, log_src, local.at[4]),
    ]
    for copy in own:
        copy.start()

    barrier = pltpu.get_barrier_semaphore()
    for d in range(1, n_tgt):
        pl.semaphore_signal(
            barrier, inc=1, device_id={"tgt": (t + d) % n_tgt}, device_id_type=pl.DeviceIdType.MESH
        )

    def greet(d, carry):
        pl.semaphore_signal(
            barrier, inc=1, device_id={"src": (s + d) % n_src}, device_id_type=pl.DeviceIdType.MESH
        )
        return carry

    lax.fori_loop(1, n_src, greet, 0)
    pl.semaphore_wait(barrier, n_src + n_tgt - 2)

    def owner_of(k, way):
        return ring_owner((place + n_src + (2 * way - 1) * k) % n_src, wide, deep)

    def ring_copy(k, way, c, first=False):
        offset = way * half + c * part
        sent = pl.multiple_of(owner_of(k - 1, way) * yb + offset, part)
        source = y_own.at[pl.ds(offset, part)] if first else y_all.at[pl.ds(sent, part)]
        return pltpu.make_async_remote_copy(
            src_ref=source,
            dst_ref=y_all.at[pl.ds(sent, part)],
            send_sem=ring_send.at[k, way, c],
            recv_sem=ring_recv.at[k, way, c],
            device_id={"src": before if way else after},
            device_id_type=pl.DeviceIdType.MESH,
        )

    def ring_arrival(k, way, c):
        offset = way * half + c * part
        got = pl.multiple_of(owner_of(k, way) * yb + offset, part)
        return pltpu.make_async_remote_copy(
            src_ref=y_all.at[pl.ds(got, part)],
            dst_ref=y_all.at[pl.ds(got, part)],
            send_sem=ring_send.at[k, way, c],
            recv_sem=ring_recv.at[k, way, c],
            device_id={"src": before if way else after},
            device_id_type=pl.DeviceIdType.MESH,
        )

    def x_copy(source, slot, send, recv, target):
        return pltpu.make_async_remote_copy(
            src_ref=source,
            dst_ref=x_all.at[slot],
            send_sem=send,
            recv_sem=recv,
            device_id={"tgt": target},
            device_id_type=pl.DeviceIdType.MESH,
        )

    order = [(way, c) for c in range(CHUNKS) for way in range(2)]
    for way, c in order:
        ring_copy(1, way, c, first=True).start()
    for d in range(1, n_y):
        target = ((y_me + d) % n_y) * 2 + core
        x_copy(x_own, t, y_send.at[d], y_recv.at[d], target).start()
    x_copy(x_own, t, core_send.at[0], core_recv.at[0], partner).start()

    for copy in own:
        copy.wait()
    a_col[...] = upright((log_tgt[...] + pot[...] / EPSILON) * LOG2E)
    row_top[...] = jnp.full_like(row_top, LOW)
    row_sum[...] = jnp.zeros_like(row_sum)

    def prepare_x(slot, values):
        where = pl.ds(pl.multiple_of(slot * xb, xb), xb)
        x_norm[where, :] = jnp.broadcast_to(jnp.sum(values * values, axis=1, keepdims=True), (xb, LANES))
        high, low = halves(values * (2.0 * scale * LOG2E))
        x_ops[where, 0:width] = high
        x_ops[where, width : 2 * width] = low
        x_ops[where, 2 * width : 3 * width] = high

    prepare_x(t, x_all[t])

    def pass_on(k, c):
        for way in range(2):
            ring_arrival(k, way, c).wait_recv()

            @pl.when(k < n_src - 1)
            def _(way=way):
                ring_copy(k + 1, way, c).start()

    def first_turns(k, carry):
        for c in range(CHUNKS):
            pass_on(k, c)
        return carry

    lax.fori_loop(1, 3, first_turns, 0)

    for d in range(1, n_y):
        slot = ((y_me + n_y - d) % n_y) * 2 + core
        x_copy(x_all.at[slot], slot, y_send.at[d], y_recv.at[d], partner).wait_recv()
        x_copy(x_all.at[slot], slot, core_send.at[d], core_recv.at[d], partner).start()
        prepare_x(slot, x_all[slot])
    for d in range(n_y):
        slot = ((y_me + n_y - d) % n_y) * 2 + 1 - core
        x_copy(x_all.at[slot], slot, core_send.at[d], core_recv.at[d], partner).wait_recv()
        prepare_x(slot, x_all[slot])

    wide_rows = min(512, rows)

    def row_sweep(first, count):
        here = pl.ds(first, count)
        values = y_all[here, :]
        norm = jnp.broadcast_to(jnp.sum(values * values, axis=1, keepdims=True), (count, LANES))
        y_norm[here, :] = norm
        bias = across(a_col[here, :] - norm * (scale * LOG2E), wide_rows)
        high, low = halves(values)
        left = jnp.concatenate([high, high, low], axis=1)
        for begin in range(0, rows, wide_rows):
            span = slice(begin, begin + wide_rows)
            product = contract(left, x_ops[span, :])
            products[here, span] = product
            scores = product + bias
            old = row_top[:, span]
            top = jnp.maximum(old, jnp.max(scores, axis=0, keepdims=True))
            total = jnp.sum(jnp.exp2(scores - top), axis=0, keepdims=True)
            row_sum[:, span] = row_sum[:, span] * jnp.exp2(old - top) + total
            row_top[:, span] = top

    def half_sweep(unit, carry):
        k, way = unit // 2, unit % 2
        row_sweep(pl.multiple_of(owner_of(k, way) * yb + way * half, half), half)
        return carry

    def turn(k, carry):
        done = jnp.minimum(CHUNKS * (k - 3), 2 * k)
        for c in range(CHUNKS):
            pass_on(k, c)
            whole = 2 if c == CHUNKS - 1 else 0
            ready = jnp.minimum(CHUNKS * (k - 3) + c + 1, 2 * k + whole)
            lax.fori_loop(done, ready, half_sweep, 0)
            done = ready
        return carry

    lax.fori_loop(3, n_src - 1, turn, 0)
    last = n_src - 1
    quarter = half // 2
    for c in range(CHUNKS):
        pass_on(last, c)
        if c % 2 == 1:
            for way in range(2):
                first = owner_of(last, way) * yb + way * half + (c // 2) * quarter
                row_sweep(pl.multiple_of(first, quarter), quarter)

    def row_copy(d, slot):
        return pltpu.make_async_remote_copy(
            src_ref=row_parts.at[slot],
            dst_ref=row_parts.at[slot],
            send_sem=row_send.at[d],
            recv_sem=row_recv.at[d],
            device_id={"tgt": (t + d) % n_tgt},
            device_id_type=pl.DeviceIdType.MESH,
        )

    row_parts[t] = row_top[...] + jnp.log2(row_sum[...])
    for d in range(1, n_tgt):
        row_copy(d, t).start()
    norms = flat(x_norm[...])
    for d in range(1, n_tgt):
        row_copy(d, (t + n_tgt - d) % n_tgt).wait_recv()
    lse = combine(row_parts, n_tgt)
    b_rows[...] = jnp.broadcast_to(log_src[...] * LOG2E - lse, b_rows.shape)
    src_out[...] = norms / width - (EPSILON * LN2) * lse

    group = min(256, cols // PARTS)

    def column_sweep(index, carry):
        begin = pl.multiple_of(index * group, group)
        tops, totals = [], []
        for first in range(0, group, 8):
            here = pl.ds(pl.multiple_of(begin + first, 8), 8)
            scores = [
                products[here, at : at + LANES] + b_rows[:, at : at + LANES]
                for at in range(0, rows, LANES)
            ]
            top = functools.reduce(jnp.maximum, scores)
            tops.append(top)
            totals.append(sum(jnp.exp2(score - top) for score in scores))
        lane_top = jnp.transpose(jnp.concatenate(tops, axis=0))
        lane_total = jnp.transpose(jnp.concatenate(totals, axis=0))
        top = jnp.max(lane_top, axis=0, keepdims=True)
        total = jnp.sum(lane_total * jnp.exp2(lane_top - top), axis=0, keepdims=True)
        col_parts[s, :, pl.ds(begin, group)] = top + jnp.log2(total)
        return carry

    share = cols // PARTS

    def col_copy(d, slot, h):
        span = pl.ds(h * share, share)
        return pltpu.make_async_remote_copy(
            src_ref=col_parts.at[slot, :, span],
            dst_ref=col_parts.at[slot, :, span],
            send_sem=col_send.at[d, h],
            recv_sem=col_recv.at[d, h],
            device_id={"src": (s + d) % n_src},
            device_id_type=pl.DeviceIdType.MESH,
        )

    for h in range(PARTS):
        lax.fori_loop(h * share // group, (h + 1) * share // group, column_sweep, 0)

        def send_columns(d, carry, h=h):
            col_copy(d, s, h).start()
            return carry

        lax.fori_loop(1, n_src, send_columns, 0)

    def take_columns(d, carry):
        for h in range(PARTS):
            col_copy(d, (s + n_src - d) % n_src, h).wait_recv()
        return carry

    norms = flat(y_norm[...])
    lax.fori_loop(1, n_src, take_columns, 0)
    tgt_out[...] = norms / width - (EPSILON * LN2) * combine(col_parts, n_src)

    def settle_ring(k, carry):
        for way, c in order:
            ring_copy(k, way, c).wait_send()
        return carry

    def settle_columns(d, carry):
        for h in range(PARTS):
            col_copy(d, s, h).wait_send()
        return carry

    lax.fori_loop(1, n_src, settle_ring, 0)
    lax.fori_loop(1, n_src, settle_columns, 0)
    for d in range(1, n_y):
        x_copy(x_all.at[t], t, y_send.at[d], y_recv.at[d], partner).wait_send()
    for d in range(n_y):
        x_copy(x_all.at[t], t, core_send.at[d], core_recv.at[d], partner).wait_send()
    for d in range(1, n_tgt):
        row_copy(d, t).wait_send()


def shards(n_src, n_tgt, src_embed, tgt_embed, log_src, log_tgt, tgt_pot):
    xb, width = src_embed.shape
    yb = tgt_embed.shape[0]
    rows, cols = n_tgt * xb, n_src * yb
    wide = max(w for w in range(1, n_src + 1) if n_src % w == 0 and 2 * w * w <= n_src)
    deep = n_src // wide
    sem = pltpu.SemaphoreType.DMA
    vmem = pl.BlockSpec(memory_space=pltpu.VMEM)
    f32, bf16 = jnp.float32, jnp.bfloat16
    src_dual, tgt_dual = pl.pallas_call(
        functools.partial(kernel, n_src, n_tgt, wide, deep),
        out_shape=(jax.ShapeDtypeStruct((1, rows), f32), jax.ShapeDtypeStruct((1, cols), f32)),
        in_specs=[pl.BlockSpec(memory_space=pl.ANY)] * 5,
        out_specs=(vmem, vmem),
        scratch_shapes=[
            pltpu.VMEM((n_tgt, xb, width), f32),
            pltpu.VMEM((cols, width), f32),
            pltpu.VMEM((rows, 3 * width), bf16),
            pltpu.VMEM((cols, rows), f32),
            pltpu.VMEM((cols, LANES), f32),
            pltpu.VMEM((8, rows), f32),
            pltpu.VMEM((rows, LANES), f32),
            pltpu.VMEM((cols, LANES), f32),
            pltpu.VMEM((1, rows), f32),
            pltpu.VMEM((1, cols), f32),
            pltpu.VMEM((1, cols), f32),
            pltpu.VMEM((1, rows), f32),
            pltpu.VMEM((1, rows), f32),
            pltpu.VMEM((n_tgt, 1, rows), f32),
            pltpu.VMEM((n_src, 1, cols), f32),
            sem((n_src, 2, CHUNKS)),
            sem((n_src, 2, CHUNKS)),
            sem((n_tgt // 2,)),
            sem((n_tgt // 2,)),
            sem((n_tgt // 2,)),
            sem((n_tgt // 2,)),
            sem((n_tgt,)),
            sem((n_tgt,)),
            sem((n_src, PARTS)),
            sem((n_src, PARTS)),
            sem((5,)),
        ],
        compiler_params=pltpu.CompilerParams(
            collective_id=0, has_side_effects=True, vmem_limit_bytes=60 * 1024 * 1024
        ),
        cost_estimate=pl.CostEstimate(
            flops=6 * rows * cols * width,
            bytes_accessed=4 * (rows + cols) * width,
            transcendentals=2 * rows * cols,
        ),
    )(src_embed, tgt_embed, log_src[None, :], log_tgt[None, :], tgt_pot[None, :])
    return src_dual.reshape(rows), tgt_dual.reshape(cols)


def solution(mesh):
    in_specs = (P(("src", "tgt"), None), P(("tgt", "src"), None), P("src"), P("tgt"), P("tgt"))
    out_specs = (P("src"), P("tgt"))
    body = functools.partial(shards, mesh.shape["src"], mesh.shape["tgt"])
    return jax.shard_map(body, mesh=mesh, in_specs=in_specs, out_specs=out_specs, check_vma=False)
```

```python
import functools

import jax
import jax.numpy as jnp
from jax import lax
from jax.experimental import pallas as pl
from jax.experimental.pallas import tpu as pltpu
from jax.sharding import PartitionSpec as P

EPSILON = 0.05
LOW = -1e38
LANES = 128
CHUNKS = 4
PARTS = 2


def ring_place(src, wide, deep):
    z, x = src // wide, src % wide
    return x * deep + jnp.where(x % 2 == 0, z, deep - 1 - z)


def ring_owner(place, wide, deep):
    x, step = place // deep, place % deep
    z = jnp.where(x % 2 == 0, step, deep - 1 - step)
    return z * wide + x


def across(column, count):
    return jnp.concatenate([column] * (count // LANES), axis=1)


def upright(row):
    return jnp.transpose(jnp.broadcast_to(row, (LANES, row.shape[1])))


def flat(columns):
    return jnp.transpose(columns)[0:1, :]


def halves(values):
    high = values.astype(jnp.bfloat16)
    low = (values - high.astype(jnp.float32)).astype(jnp.bfloat16)
    return high, low


def contract(left, right):
    return lax.dot_general(
        left, right, (((1,), (1,)), ((), ())), preferred_element_type=jnp.float32
    )


def combine(parts, count):
    top = functools.reduce(jnp.maximum, [parts[k] for k in range(count)])
    total = sum(jnp.exp(parts[k] - top) for k in range(count))
    return top + jnp.log(total)


def kernel(
    n_src, n_tgt, wide, deep,
    x_own, y_own, log_src_in, log_tgt_in, pot_in, src_out, tgt_out,
    x_all, y_all, x_ops, products, a_col, b_rows, x_norm, y_norm,
    log_src, log_tgt, pot, row_top, row_sum, row_parts, col_parts,
    ring_send, ring_recv, y_send, y_recv, core_send, core_recv,
    row_send, row_recv, col_send, col_recv, local,
):
    s = lax.axis_index("src")
    t = lax.axis_index("tgt")
    n_y = n_tgt // 2
    y_me, core = t // 2, t % 2
    partner = y_me * 2 + 1 - core
    place = ring_place(s, wide, deep)
    after = ring_owner((place + 1) % n_src, wide, deep)
    before = ring_owner((place + n_src - 1) % n_src, wide, deep)
    xb, width = x_own.shape
    yb = y_own.shape[0]
    rows, cols = n_tgt * xb, n_src * yb
    half = yb // 2
    part = half // CHUNKS
    scale = 1.0 / (width * EPSILON)

    own_rows = pl.ds(pl.multiple_of(s * yb, yb), yb)
    own = [
        pltpu.make_async_copy(log_tgt_in, log_tgt, local.at[0]),
        pltpu.make_async_copy(pot_in, pot, local.at[1]),
        pltpu.make_async_copy(x_own, x_all.at[t], local.at[2]),
        pltpu.make_async_copy(y_own, y_all.at[own_rows], local.at[3]),
        pltpu.make_async_copy(log_src_in, log_src, local.at[4]),
    ]
    for copy in own:
        copy.start()

    barrier = pltpu.get_barrier_semaphore()
    for d in range(1, n_tgt):
        pl.semaphore_signal(
            barrier, inc=1, device_id={"tgt": (t + d) % n_tgt}, device_id_type=pl.DeviceIdType.MESH
        )

    def greet(d, carry):
        pl.semaphore_signal(
            barrier, inc=1, device_id={"src": (s + d) % n_src}, device_id_type=pl.DeviceIdType.MESH
        )
        return carry

    lax.fori_loop(1, n_src, greet, 0)
    pl.semaphore_wait(barrier, n_src + n_tgt - 2)

    def owner_of(k, way):
        return ring_owner((place + n_src + (2 * way - 1) * k) % n_src, wide, deep)

    def ring_copy(k, way, c, first=False):
        offset = way * half + c * part
        sent = pl.multiple_of(owner_of(k - 1, way) * yb + offset, part)
        source = y_own.at[pl.ds(offset, part)] if first else y_all.at[pl.ds(sent, part)]
        return pltpu.make_async_remote_copy(
            src_ref=source,
            dst_ref=y_all.at[pl.ds(sent, part)],
            send_sem=ring_send.at[k, way, c],
            recv_sem=ring_recv.at[k, way, c],
            device_id={"src": before if way else after},
            device_id_type=pl.DeviceIdType.MESH,
        )

    def ring_arrival(k, way, c):
        offset = way * half + c * part
        got = pl.multiple_of(owner_of(k, way) * yb + offset, part)
        return pltpu.make_async_remote_copy(
            src_ref=y_all.at[pl.ds(got, part)],
            dst_ref=y_all.at[pl.ds(got, part)],
            send_sem=ring_send.at[k, way, c],
            recv_sem=ring_recv.at[k, way, c],
            device_id={"src": before if way else after},
            device_id_type=pl.DeviceIdType.MESH,
        )

    def x_copy(source, slot, send, recv, target):
        return pltpu.make_async_remote_copy(
            src_ref=source,
            dst_ref=x_all.at[slot],
            send_sem=send,
            recv_sem=recv,
            device_id={"tgt": target},
            device_id_type=pl.DeviceIdType.MESH,
        )

    order = [(way, c) for c in range(CHUNKS) for way in range(2)]
    for way, c in order:
        ring_copy(1, way, c, first=True).start()
    for d in range(1, n_y):
        target = ((y_me + d) % n_y) * 2 + core
        x_copy(x_own, t, y_send.at[d], y_recv.at[d], target).start()
    x_copy(x_own, t, core_send.at[0], core_recv.at[0], partner).start()

    for copy in own:
        copy.wait()
    a_col[...] = upright(log_tgt[...] + pot[...] / EPSILON)
    row_top[...] = jnp.full_like(row_top, LOW)
    row_sum[...] = jnp.zeros_like(row_sum)

    def prepare_x(slot, values):
        where = pl.ds(pl.multiple_of(slot * xb, xb), xb)
        x_norm[where, :] = jnp.broadcast_to(jnp.sum(values * values, axis=1, keepdims=True), (xb, LANES))
        high, low = halves(values * (2.0 * scale))
        x_ops[where, 0:width] = high
        x_ops[where, width : 2 * width] = low
        x_ops[where, 2 * width : 3 * width] = high

    prepare_x(t, x_all[t])

    near = [t, partner]
    far = [((y_me + d) % n_y) * 2 + c for d in range(1, n_y) for c in range(2)]

    def row_sweep(first, count, slots):
        here = pl.ds(first, count)
        values = y_all[here, :]
        norm = jnp.broadcast_to(jnp.sum(values * values, axis=1, keepdims=True), (count, LANES))
        y_norm[here, :] = norm
        bias = across(a_col[here, :] - norm * scale, xb)
        high, low = halves(values)
        left = jnp.concatenate([high, high, low], axis=1)
        for slot in slots:
            span = pl.ds(pl.multiple_of(slot * xb, xb), xb)
            product = contract(left, x_ops[span, :])
            products[here, span] = product
            scores = product + bias
            old = row_top[:, span]
            top = jnp.maximum(old, jnp.max(scores, axis=0, keepdims=True))
            total = jnp.sum(jnp.exp(scores - top), axis=0, keepdims=True)
            row_sum[:, span] = row_sum[:, span] * jnp.exp(old - top) + total
            row_top[:, span] = top

    def half_first(k, way):
        return pl.multiple_of(owner_of(k, way) * yb + way * half, half)

    def early_sweep(unit, carry):
        row_sweep(half_first(unit // 2, unit % 2), half, near)
        return carry

    def pass_on(k, c):
        for way in range(2):
            ring_arrival(k, way, c).wait_recv()

            @pl.when(k < n_src - 1)
            def _(way=way):
                ring_copy(k + 1, way, c).start()

    def first_turns(k, carry):
        lax.fori_loop(2 * (k - 1), 2 * k, early_sweep, 0)
        for c in range(CHUNKS):
            pass_on(k, c)
        return carry

    x_copy(x_all.at[partner], partner, core_send.at[0], core_recv.at[0], partner).wait_recv()
    prepare_x(partner, x_all[partner])
    lax.fori_loop(1, 3, first_turns, 0)
    lax.fori_loop(4, 6, early_sweep, 0)

    for d in range(1, n_y):
        slot = ((y_me + n_y - d) % n_y) * 2 + core
        x_copy(x_all.at[slot], slot, y_send.at[d], y_recv.at[d], partner).wait_recv()
        x_copy(x_all.at[slot], slot, core_send.at[d], core_recv.at[d], partner).start()
        prepare_x(slot, x_all[slot])
    for d in range(1, n_y):
        slot = ((y_me + n_y - d) % n_y) * 2 + 1 - core
        x_copy(x_all.at[slot], slot, core_send.at[d], core_recv.at[d], partner).wait_recv()
        prepare_x(slot, x_all[slot])

    def half_sweep(unit, carry):
        k, way = unit // 2, unit % 2

        @pl.when(k < 3)
        def _():
            row_sweep(half_first(k, way), half, far)

        @pl.when(k >= 3)
        def _():
            row_sweep(half_first(k, way), half, near + far)

        return carry

    def turn(k, carry):
        done = jnp.minimum(CHUNKS * (k - 3), 2 * k)
        for c in range(CHUNKS):
            pass_on(k, c)
            whole = 2 if c == CHUNKS - 1 else 0
            ready = jnp.minimum(CHUNKS * (k - 3) + c + 1, 2 * k + whole)
            lax.fori_loop(done, ready, half_sweep, 0)
            done = ready
        return carry

    lax.fori_loop(3, n_src - 1, turn, 0)
    last = n_src - 1
    quarter = half // 2
    for c in range(CHUNKS):
        pass_on(last, c)
        if c % 2 == 1:
            for way in range(2):
                first = owner_of(last, way) * yb + way * half + (c // 2) * quarter
                row_sweep(pl.multiple_of(first, quarter), quarter, near + far)

    def row_copy(d, slot):
        return pltpu.make_async_remote_copy(
            src_ref=row_parts.at[slot],
            dst_ref=row_parts.at[slot],
            send_sem=row_send.at[d],
            recv_sem=row_recv.at[d],
            device_id={"tgt": (t + d) % n_tgt},
            device_id_type=pl.DeviceIdType.MESH,
        )

    row_parts[t] = row_top[...] + jnp.log(row_sum[...])
    for d in range(1, n_tgt):
        row_copy(d, t).start()
    norms = flat(x_norm[...])
    for d in range(1, n_tgt):
        row_copy(d, (t + n_tgt - d) % n_tgt).wait_recv()
    lse = combine(row_parts, n_tgt)
    b_rows[...] = jnp.broadcast_to(log_src[...] - lse, b_rows.shape)
    src_out[...] = norms / width - EPSILON * lse

    group = min(256, cols // PARTS)

    def column_sweep(index, carry):
        begin = pl.multiple_of(index * group, group)
        tops, totals = [], []
        for first in range(0, group, 8):
            here = pl.ds(pl.multiple_of(begin + first, 8), 8)
            scores = [
                products[here, at : at + LANES] + b_rows[:, at : at + LANES]
                for at in range(0, rows, LANES)
            ]
            top = functools.reduce(jnp.maximum, scores)
            tops.append(top)
            totals.append(sum(jnp.exp(score - top) for score in scores))
        lane_top = jnp.transpose(jnp.concatenate(tops, axis=0))
        lane_total = jnp.transpose(jnp.concatenate(totals, axis=0))
        top = jnp.max(lane_top, axis=0, keepdims=True)
        total = jnp.sum(lane_total * jnp.exp(lane_top - top), axis=0, keepdims=True)
        col_parts[s, :, pl.ds(begin, group)] = top + jnp.log(total)
        return carry

    share = cols // PARTS

    def col_copy(d, slot, h):
        span = pl.ds(h * share, share)
        return pltpu.make_async_remote_copy(
            src_ref=col_parts.at[slot, :, span],
            dst_ref=col_parts.at[slot, :, span],
            send_sem=col_send.at[d, h],
            recv_sem=col_recv.at[d, h],
            device_id={"src": (s + d) % n_src},
            device_id_type=pl.DeviceIdType.MESH,
        )

    for h in range(PARTS):
        lax.fori_loop(h * share // group, (h + 1) * share // group, column_sweep, 0)

        def send_columns(d, carry, h=h):
            col_copy(d, s, h).start()
            return carry

        lax.fori_loop(1, n_src, send_columns, 0)

    def take_columns(d, carry):
        for h in range(PARTS):
            col_copy(d, (s + n_src - d) % n_src, h).wait_recv()
        return carry

    norms = flat(y_norm[...])
    lax.fori_loop(1, n_src, take_columns, 0)
    tgt_out[...] = norms / width - EPSILON * combine(col_parts, n_src)

    def settle_ring(k, carry):
        for way, c in order:
            ring_copy(k, way, c).wait_send()
        return carry

    def settle_columns(d, carry):
        for h in range(PARTS):
            col_copy(d, s, h).wait_send()
        return carry

    lax.fori_loop(1, n_src, settle_ring, 0)
    lax.fori_loop(1, n_src, settle_columns, 0)
    for d in range(1, n_y):
        x_copy(x_all.at[t], t, y_send.at[d], y_recv.at[d], partner).wait_send()
    for d in range(n_y):
        x_copy(x_all.at[t], t, core_send.at[d], core_recv.at[d], partner).wait_send()
    for d in range(1, n_tgt):
        row_copy(d, t).wait_send()


def shards(n_src, n_tgt, src_embed, tgt_embed, log_src, log_tgt, tgt_pot):
    xb, width = src_embed.shape
    yb = tgt_embed.shape[0]
    rows, cols = n_tgt * xb, n_src * yb
    wide = max(w for w in range(1, n_src + 1) if n_src % w == 0 and 2 * w * w <= n_src)
    deep = n_src // wide
    sem = pltpu.SemaphoreType.DMA
    vmem = pl.BlockSpec(memory_space=pltpu.VMEM)
    f32, bf16 = jnp.float32, jnp.bfloat16
    src_dual, tgt_dual = pl.pallas_call(
        functools.partial(kernel, n_src, n_tgt, wide, deep),
        out_shape=(jax.ShapeDtypeStruct((1, rows), f32), jax.ShapeDtypeStruct((1, cols), f32)),
        in_specs=[pl.BlockSpec(memory_space=pl.ANY)] * 5,
        out_specs=(vmem, vmem),
        scratch_shapes=[
            pltpu.VMEM((n_tgt, xb, width), f32),
            pltpu.VMEM((cols, width), f32),
            pltpu.VMEM((rows, 3 * width), bf16),
            pltpu.VMEM((cols, rows), f32),
            pltpu.VMEM((cols, LANES), f32),
            pltpu.VMEM((8, rows), f32),
            pltpu.VMEM((rows, LANES), f32),
            pltpu.VMEM((cols, LANES), f32),
            pltpu.VMEM((1, rows), f32),
            pltpu.VMEM((1, cols), f32),
            pltpu.VMEM((1, cols), f32),
            pltpu.VMEM((1, rows), f32),
            pltpu.VMEM((1, rows), f32),
            pltpu.VMEM((n_tgt, 1, rows), f32),
            pltpu.VMEM((n_src, 1, cols), f32),
            sem((n_src, 2, CHUNKS)),
            sem((n_src, 2, CHUNKS)),
            sem((n_tgt // 2,)),
            sem((n_tgt // 2,)),
            sem((n_tgt // 2,)),
            sem((n_tgt // 2,)),
            sem((n_tgt,)),
            sem((n_tgt,)),
            sem((n_src, PARTS)),
            sem((n_src, PARTS)),
            sem((5,)),
        ],
        compiler_params=pltpu.CompilerParams(
            collective_id=0, has_side_effects=True, vmem_limit_bytes=60 * 1024 * 1024
        ),
        cost_estimate=pl.CostEstimate(
            flops=6 * rows * cols * width,
            bytes_accessed=4 * (rows + cols) * width,
            transcendentals=2 * rows * cols,
        ),
    )(src_embed, tgt_embed, log_src[None, :], log_tgt[None, :], tgt_pot[None, :])
    return src_dual.reshape(rows), tgt_dual.reshape(cols)


def solution(mesh):
    in_specs = (P(("src", "tgt"), None), P(("tgt", "src"), None), P("src"), P("tgt"), P("tgt"))
    out_specs = (P("src"), P("tgt"))
    body = functools.partial(shards, mesh.shape["src"], mesh.shape["tgt"])
    return jax.shard_map(body, mesh=mesh, in_specs=in_specs, out_specs=out_specs, check_vma=False)
```

```python
import functools

import jax
import jax.numpy as jnp
from jax import lax
from jax.experimental import pallas as pl
from jax.experimental.pallas import tpu as pltpu
from jax.sharding import PartitionSpec as P

EPSILON = 0.05
LOW = -1e38
LANES = 128
CHUNKS = 4
PARTS = 2


def ring_place(src, wide, deep):
    z, x = src // wide, src % wide
    return x * deep + jnp.where(x % 2 == 0, z, deep - 1 - z)


def ring_owner(place, wide, deep):
    x, step = place // deep, place % deep
    z = jnp.where(x % 2 == 0, step, deep - 1 - step)
    return z * wide + x


def across(column, count):
    return jnp.concatenate([column] * (count // LANES), axis=1)


def upright(row):
    return jnp.transpose(jnp.broadcast_to(row, (LANES, row.shape[1])))


def flat(columns):
    return jnp.transpose(columns)[0:1, :]


def halves(values):
    high = values.astype(jnp.bfloat16)
    low = (values - high.astype(jnp.float32)).astype(jnp.bfloat16)
    return high, low


def contract(left, right):
    return lax.dot_general(
        left, right, (((1,), (1,)), ((), ())), preferred_element_type=jnp.float32
    )


def combine(parts, count):
    top = functools.reduce(jnp.maximum, [parts[k] for k in range(count)])
    total = sum(jnp.exp(parts[k] - top) for k in range(count))
    return top + jnp.log(total)


def kernel(
    n_src, n_tgt, wide, deep,
    x_own, y_own, log_src_in, log_tgt_in, pot_in, src_out, tgt_out,
    x_all, y_all, x_ops, products, a_col, b_rows, x_norm, y_norm,
    log_src, log_tgt, pot, row_top, row_sum, row_parts, col_parts,
    ring_send, ring_recv, y_send, y_recv, core_send, core_recv,
    row_send, row_recv, col_send, col_recv, local,
):
    s = lax.axis_index("src")
    t = lax.axis_index("tgt")
    n_y = n_tgt // 2
    y_me, core = t // 2, t % 2
    partner = y_me * 2 + 1 - core
    place = ring_place(s, wide, deep)
    after = ring_owner((place + 1) % n_src, wide, deep)
    before = ring_owner((place + n_src - 1) % n_src, wide, deep)
    xb, width = x_own.shape
    yb = y_own.shape[0]
    rows, cols = n_tgt * xb, n_src * yb
    half = yb // 2
    part = half // CHUNKS
    scale = 1.0 / (width * EPSILON)

    own_rows = pl.ds(pl.multiple_of(s * yb, yb), yb)
    own = [
        pltpu.make_async_copy(log_tgt_in, log_tgt, local.at[0]),
        pltpu.make_async_copy(pot_in, pot, local.at[1]),
        pltpu.make_async_copy(x_own, x_all.at[t], local.at[2]),
        pltpu.make_async_copy(y_own, y_all.at[own_rows], local.at[3]),
        pltpu.make_async_copy(log_src_in, log_src, local.at[4]),
    ]
    for copy in own:
        copy.start()

    barrier = pltpu.get_barrier_semaphore()
    for d in range(1, n_tgt):
        pl.semaphore_signal(
            barrier, inc=1, device_id={"tgt": (t + d) % n_tgt}, device_id_type=pl.DeviceIdType.MESH
        )

    def greet(d, carry):
        pl.semaphore_signal(
            barrier, inc=1, device_id={"src": (s + d) % n_src}, device_id_type=pl.DeviceIdType.MESH
        )
        return carry

    lax.fori_loop(1, n_src, greet, 0)
    pl.semaphore_wait(barrier, n_src + n_tgt - 2)

    def owner_of(k, way):
        return ring_owner((place + n_src + (2 * way - 1) * k) % n_src, wide, deep)

    def ring_copy(k, way, c, first=False):
        offset = way * half + c * part
        sent = pl.multiple_of(owner_of(k - 1, way) * yb + offset, part)
        source = y_own.at[pl.ds(offset, part)] if first else y_all.at[pl.ds(sent, part)]
        return pltpu.make_async_remote_copy(
            src_ref=source,
            dst_ref=y_all.at[pl.ds(sent, part)],
            send_sem=ring_send.at[k, way, c],
            recv_sem=ring_recv.at[k, way, c],
            device_id={"src": before if way else after},
            device_id_type=pl.DeviceIdType.MESH,
        )

    def ring_arrival(k, way, c):
        offset = way * half + c * part
        got = pl.multiple_of(owner_of(k, way) * yb + offset, part)
        return pltpu.make_async_remote_copy(
            src_ref=y_all.at[pl.ds(got, part)],
            dst_ref=y_all.at[pl.ds(got, part)],
            send_sem=ring_send.at[k, way, c],
            recv_sem=ring_recv.at[k, way, c],
            device_id={"src": before if way else after},
            device_id_type=pl.DeviceIdType.MESH,
        )

    def x_copy(source, slot, send, recv, target):
        return pltpu.make_async_remote_copy(
            src_ref=source,
            dst_ref=x_all.at[slot],
            send_sem=send,
            recv_sem=recv,
            device_id={"tgt": target},
            device_id_type=pl.DeviceIdType.MESH,
        )

    order = [(way, c) for c in range(CHUNKS) for way in range(2)]
    for way, c in order:
        ring_copy(1, way, c, first=True).start()
    for d in range(1, n_y):
        target = ((y_me + d) % n_y) * 2 + core
        x_copy(x_own, t, y_send.at[d], y_recv.at[d], target).start()
    x_copy(x_own, t, core_send.at[0], core_recv.at[0], partner).start()

    for copy in own:
        copy.wait()
    a_col[...] = upright((log_tgt[...] + pot[...] / EPSILON))
    row_top[...] = jnp.full_like(row_top, LOW)
    row_sum[...] = jnp.zeros_like(row_sum)

    def prepare_x(slot, values):
        where = pl.ds(pl.multiple_of(slot * xb, xb), xb)
        x_norm[where, :] = jnp.broadcast_to(jnp.sum(values * values, axis=1, keepdims=True), (xb, LANES))
        high, low = halves(values * (2.0 * scale))
        x_ops[where, 0:width] = high
        x_ops[where, width : 2 * width] = low
        x_ops[where, 2 * width : 3 * width] = high

    prepare_x(t, x_all[t])

    def pass_on(k, c):
        for way in range(2):
            ring_arrival(k, way, c).wait_recv()

            @pl.when(k < n_src - 1)
            def _(way=way):
                ring_copy(k + 1, way, c).start()

    def first_turns(k, carry):
        for c in range(CHUNKS):
            pass_on(k, c)
        return carry

    lax.fori_loop(1, 3, first_turns, 0)

    for d in range(1, n_y):
        slot = ((y_me + n_y - d) % n_y) * 2 + core
        x_copy(x_all.at[slot], slot, y_send.at[d], y_recv.at[d], partner).wait_recv()
        x_copy(x_all.at[slot], slot, core_send.at[d], core_recv.at[d], partner).start()
        prepare_x(slot, x_all[slot])
    for d in range(n_y):
        slot = ((y_me + n_y - d) % n_y) * 2 + 1 - core
        x_copy(x_all.at[slot], slot, core_send.at[d], core_recv.at[d], partner).wait_recv()
        prepare_x(slot, x_all[slot])

    wide_rows = min(512, rows)

    def row_sweep(first, count):
        here = pl.ds(first, count)
        values = y_all[here, :]
        norm = jnp.broadcast_to(jnp.sum(values * values, axis=1, keepdims=True), (count, LANES))
        y_norm[here, :] = norm
        bias = across(a_col[here, :] - norm * (scale), wide_rows)
        high, low = halves(values)
        left = jnp.concatenate([high, high, low], axis=1)
        for begin in range(0, rows, wide_rows):
            span = slice(begin, begin + wide_rows)
            product = contract(left, x_ops[span, :])
            products[here, span] = product
            scores = product + bias
            old = row_top[:, span]
            top = jnp.maximum(old, jnp.max(scores, axis=0, keepdims=True))
            total = jnp.sum(jnp.exp(scores - top), axis=0, keepdims=True)
            row_sum[:, span] = row_sum[:, span] * jnp.exp(old - top) + total
            row_top[:, span] = top

    def half_sweep(unit, carry):
        k, way = unit // 2, unit % 2
        row_sweep(pl.multiple_of(owner_of(k, way) * yb + way * half, half), half)
        return carry

    def turn(k, carry):
        done = jnp.minimum(CHUNKS * (k - 3), 2 * k)
        for c in range(CHUNKS):
            pass_on(k, c)
            whole = 2 if c == CHUNKS - 1 else 0
            ready = jnp.minimum(CHUNKS * (k - 3) + c + 1, 2 * k + whole)
            lax.fori_loop(done, ready, half_sweep, 0)
            done = ready
        return carry

    lax.fori_loop(3, n_src - 1, turn, 0)
    last = n_src - 1
    quarter = half // 2
    for c in range(CHUNKS):
        pass_on(last, c)
        if c % 2 == 1:
            for way in range(2):
                first = owner_of(last, way) * yb + way * half + (c // 2) * quarter
                row_sweep(pl.multiple_of(first, quarter), quarter)

    def row_copy(d, slot):
        return pltpu.make_async_remote_copy(
            src_ref=row_parts.at[slot],
            dst_ref=row_parts.at[slot],
            send_sem=row_send.at[d],
            recv_sem=row_recv.at[d],
            device_id={"tgt": (t + d) % n_tgt},
            device_id_type=pl.DeviceIdType.MESH,
        )

    row_parts[t] = row_top[...] + jnp.log(row_sum[...])
    for d in range(1, n_tgt):
        row_copy(d, t).start()
    norms = flat(x_norm[...])
    for d in range(1, n_tgt):
        row_copy(d, (t + n_tgt - d) % n_tgt).wait_recv()
    lse = combine(row_parts, n_tgt)
    b_rows[...] = jnp.broadcast_to(log_src[...] - lse, b_rows.shape)
    src_out[...] = norms / width - EPSILON * lse

    group = min(256, cols // PARTS)

    def column_sweep(index, carry):
        begin = pl.multiple_of(index * group, group)
        tops, totals = [], []
        for first in range(0, group, 8):
            here = pl.ds(pl.multiple_of(begin + first, 8), 8)
            scores = [
                products[here, at : at + LANES] + b_rows[:, at : at + LANES]
                for at in range(0, rows, LANES)
            ]
            top = functools.reduce(jnp.maximum, scores)
            tops.append(top)
            totals.append(sum(jnp.exp(score - top) for score in scores))
        lane_top = jnp.transpose(jnp.concatenate(tops, axis=0))
        lane_total = jnp.transpose(jnp.concatenate(totals, axis=0))
        top = jnp.max(lane_top, axis=0, keepdims=True)
        total = jnp.sum(lane_total * jnp.exp(lane_top - top), axis=0, keepdims=True)
        col_parts[s, :, pl.ds(begin, group)] = top + jnp.log(total)
        return carry

    share = cols // PARTS

    def col_copy(d, slot, h):
        span = pl.ds(h * share, share)
        return pltpu.make_async_remote_copy(
            src_ref=col_parts.at[slot, :, span],
            dst_ref=col_parts.at[slot, :, span],
            send_sem=col_send.at[d, h],
            recv_sem=col_recv.at[d, h],
            device_id={"src": (s + d) % n_src},
            device_id_type=pl.DeviceIdType.MESH,
        )

    for h in range(PARTS):
        lax.fori_loop(h * share // group, (h + 1) * share // group, column_sweep, 0)

        def send_columns(d, carry, h=h):
            col_copy(d, s, h).start()
            return carry

        lax.fori_loop(1, n_src, send_columns, 0)

    def take_columns(d, carry):
        for h in range(PARTS):
            col_copy(d, (s + n_src - d) % n_src, h).wait_recv()
        return carry

    norms = flat(y_norm[...])
    lax.fori_loop(1, n_src, take_columns, 0)
    tgt_out[...] = norms / width - EPSILON * combine(col_parts, n_src)

    def settle_ring(k, carry):
        for way, c in order:
            ring_copy(k, way, c).wait_send()
        return carry

    def settle_columns(d, carry):
        for h in range(PARTS):
            col_copy(d, s, h).wait_send()
        return carry

    lax.fori_loop(1, n_src, settle_ring, 0)
    lax.fori_loop(1, n_src, settle_columns, 0)
    for d in range(1, n_y):
        x_copy(x_all.at[t], t, y_send.at[d], y_recv.at[d], partner).wait_send()
    for d in range(n_y):
        x_copy(x_all.at[t], t, core_send.at[d], core_recv.at[d], partner).wait_send()
    for d in range(1, n_tgt):
        row_copy(d, t).wait_send()


def shards(n_src, n_tgt, src_embed, tgt_embed, log_src, log_tgt, tgt_pot):
    xb, width = src_embed.shape
    yb = tgt_embed.shape[0]
    rows, cols = n_tgt * xb, n_src * yb
    wide = max(w for w in range(1, n_src + 1) if n_src % w == 0 and 2 * w * w <= n_src)
    deep = n_src // wide
    sem = pltpu.SemaphoreType.DMA
    vmem = pl.BlockSpec(memory_space=pltpu.VMEM)
    f32, bf16 = jnp.float32, jnp.bfloat16
    src_dual, tgt_dual = pl.pallas_call(
        functools.partial(kernel, n_src, n_tgt, wide, deep),
        out_shape=(jax.ShapeDtypeStruct((1, rows), f32), jax.ShapeDtypeStruct((1, cols), f32)),
        in_specs=[pl.BlockSpec(memory_space=pl.ANY)] * 5,
        out_specs=(vmem, vmem),
        scratch_shapes=[
            pltpu.VMEM((n_tgt, xb, width), f32),
            pltpu.VMEM((cols, width), f32),
            pltpu.VMEM((rows, 3 * width), bf16),
            pltpu.VMEM((cols, rows), f32),
            pltpu.VMEM((cols, LANES), f32),
            pltpu.VMEM((8, rows), f32),
            pltpu.VMEM((rows, LANES), f32),
            pltpu.VMEM((cols, LANES), f32),
            pltpu.VMEM((1, rows), f32),
            pltpu.VMEM((1, cols), f32),
            pltpu.VMEM((1, cols), f32),
            pltpu.VMEM((1, rows), f32),
            pltpu.VMEM((1, rows), f32),
            pltpu.VMEM((n_tgt, 1, rows), f32),
            pltpu.VMEM((n_src, 1, cols), f32),
            sem((n_src, 2, CHUNKS)),
            sem((n_src, 2, CHUNKS)),
            sem((n_tgt // 2,)),
            sem((n_tgt // 2,)),
            sem((n_tgt // 2,)),
            sem((n_tgt // 2,)),
            sem((n_tgt,)),
            sem((n_tgt,)),
            sem((n_src, PARTS)),
            sem((n_src, PARTS)),
            sem((5,)),
        ],
        compiler_params=pltpu.CompilerParams(
            collective_id=0, has_side_effects=True, vmem_limit_bytes=60 * 1024 * 1024
        ),
        cost_estimate=pl.CostEstimate(
            flops=6 * rows * cols * width,
            bytes_accessed=4 * (rows + cols) * width,
            transcendentals=2 * rows * cols,
        ),
    )(src_embed, tgt_embed, log_src[None, :], log_tgt[None, :], tgt_pot[None, :])
    return src_dual.reshape(rows), tgt_dual.reshape(cols)


def solution(mesh):
    in_specs = (P(("src", "tgt"), None), P(("tgt", "src"), None), P("src"), P("tgt"), P("tgt"))
    out_specs = (P("src"), P("tgt"))
    body = functools.partial(shards, mesh.shape["src"], mesh.shape["tgt"])
    return jax.shard_map(body, mesh=mesh, in_specs=in_specs, out_specs=out_specs, check_vma=False)
```
